512 devices in a mesh: dp: 128 (over x, z, y_hi), grp: 4 (over y_lo, core).
Axes of the slice: x: 4, y: 8 (y_hi: 4, y_lo: 2; y = y_hi * 2 + y_lo), z: 8, core: 2. Of those that a mesh axis runs over, the one named last changes fastest.
Arguments:
- master: float32 [4, 512, 8192], P('grp', 'dp'), may hold values from -6 to 6
- first_moment: float32 [4, 512, 8192], P('grp', 'dp'), may hold values from -0.03 to 0.03
- second_moment: float32 [4, 512, 8192], P('grp', 'dp'), may hold values from 1e-05 to 0.01
- gradient: bfloat16 [4, 512, 8192], P('grp', 'dp'), may hold values from -0.29882812 to 0.29882812
- checkpoints: float32 [3, 4, 128, 2, 12, 2048], P(None, 'grp', 'dp'), as said below
- block_holder: int32 [4, 128, 16], P('grp', 'dp'), may hold values from 1 to 2, as said below
- failed_member: int32 [128], P('dp'), may hold values from 0 to 3
Outputs:
- new_master: float32 [4, 512, 8192], P('grp', 'dp')
- new_first: float32 [4, 512, 8192], P('grp', 'dp')
- new_second: float32 [4, 512, 8192], P('grp', 'dp')
- weights: bfloat16 [4, 512, 8192], P('grp')
The draws below stay inside these ranges and needn't reach their ends.
Inputs may be any that keep to these rules, and one draw needn't show every extreme that they name: `block_holder`: each value is 1 or 2. For every shard, at most 12 blocks carry each value, and at each dp index some shard has exactly 12 blocks with value 1. The checkpoint slots of a holder for a source are filled in increasing block order; slots past the count hold stale data. `checkpoints`: row 0 holds master values, row 1 first moments, row 2 second moments, positive.
All inputs are finite; a program needn't handle non-finite values.
Results may differ from the reference program's by a relative error of at most 0.005.
Values may be sent and summed in bfloat16 or wider, within the bound.
A program may use at most 64 MiB of HBM per device.

```python
import math
import jax
import jax.numpy as jnp

D = 8192
ROWS_DEV = 4
BLOCKS = 16
OFFSETS = 2
MOST = 12
BLK = 2048
ROWS = 512
N_DP = 128
N_GRP = 4


def draw_checkpoints(key, part):
    key = jax.random.fold_in(key, 2)
    shape = (N_GRP, N_DP, OFFSETS, MOST, BLK)
    keys = jax.random.split(key, 3)
    master_rows = jnp.clip(jax.random.normal(keys[0], shape, jnp.float32), -6.0, 6.0)
    first_rows = jnp.clip(0.005 * jax.random.normal(keys[1], shape, jnp.float32), -0.03, 0.03)
    logs = jax.random.uniform(keys[2], shape, jnp.float32, jnp.log(1e-05), jnp.log(0.01))
    second_rows = jnp.exp(logs)
    return jnp.stack([master_rows, first_rows, second_rows], axis=0)


def draw_block_holder(key, part):
    key = jax.random.fold_in(key, 1)
    keys = jax.random.split(key, 3)
    counts = jax.random.randint(keys[0], (N_GRP, N_DP), BLOCKS - MOST, MOST + 1)
    chosen = jax.random.randint(keys[1], (N_DP,), 0, N_GRP)
    member_ids = jnp.arange(N_GRP, dtype=jnp.int32)[:, None]
    counts = jnp.where(member_ids == chosen[None, :], MOST, counts)
    scores = jax.random.randint(keys[2], (N_GRP, N_DP, BLOCKS), 0, 1 << 20) * BLOCKS + jnp.arange(BLOCKS, dtype=jnp.int32)
    ranks = jnp.argsort(jnp.argsort(scores, axis=-1, stable=True), axis=-1, stable=True)
    return jnp.where(ranks < counts[:, :, None], 1, 2).astype(jnp.int32)


def place_ends(values, key, least, high):
    extent = values.shape
    place = [jax.random.randint(jax.random.fold_in(key, axis), (), 0, extent[axis]) for axis in range(len(extent))]
    values = values.at[tuple(place)].set(least)
    longest = extent.index(max(extent))
    place[longest] = (place[longest] + 1) % extent[longest]
    return values.at[tuple(place)].set(high)


def block_scale(own_key, extent, shards, smallest, high):
    factor_of, own = 1.0, jax.random.fold_in(own_key, 6)
    for position, blocks in shards:
        draws = jnp.exp(jax.random.uniform(jax.random.fold_in(own, position), (blocks,), jnp.float32, smallest / len(shards), high / len(shards)))
        factor_of = factor_of * jnp.repeat(draws, extent[position] // blocks).reshape([-1 if axis == position else 1 for axis in range(len(extent))])
    return factor_of


def centred(rng, extent, scale, most, shards=(), held_as=jnp.bfloat16):
    factor_of = block_scale(rng, extent, shards, -0.22, 0.18) if shards else 1.0
    array = jax.random.normal(rng, extent, jnp.float32) * scale * factor_of
    return jnp.minimum(jnp.maximum(array, -most), most).astype(held_as)


def setup_inputs(seed: int = 0) -> dict:
    splits = jax.random.split(jax.random.key(seed), 8)
    return {
        "master": centred(splits[0], (N_GRP, ROWS, D), 1.0, 6.0, ((0, 4), (1, 128)), jnp.float32),
        "first_moment": centred(splits[1], (N_GRP, ROWS, D), 0.005, 0.03, ((0, 4), (1, 128)), jnp.float32),
        "second_moment": jnp.clip(jnp.exp(math.log(0.01) - 6.9077553 * jax.random.uniform(splits[2], (N_GRP, ROWS, D), jnp.float32) ** block_scale(splits[2], (N_GRP, ROWS, D), ((0, 4), (1, 128)), -0.2, 0.2)), 9.999999747378752e-06, 0.01),
        "gradient": centred(splits[3], (N_GRP, ROWS, D), 0.05, 0.29882812, ((0, 4), (1, 128))),
        "checkpoints": draw_checkpoints(jax.random.fold_in(splits[7], 71), 0),
        "block_holder": draw_block_holder(jax.random.fold_in(splits[7], 71), 0),
        "failed_member": place_ends(jax.random.randint(splits[6], (N_DP,), 0, N_GRP), jax.random.fold_in(splits[6], 1), 0, N_GRP - 1).astype(jnp.int32),
    }


beta_one = 0.9
beta_two = 0.95
learning_rate = 0.05
weight_decay = 0.1
epsilon = 1e-08
correct_one = 1.0 - 0.9 ** 10
correct_two = 1.0 - 0.95 ** 10

def adamw_step(master, first, second, gradient):
    grad_float = gradient.astype(jnp.float32)
    new_first = beta_one * first + (1.0 - beta_one) * grad_float
    new_second = beta_two * second + (1.0 - beta_two) * grad_float * grad_float
    update = new_first / correct_one / (jnp.sqrt(new_second / correct_two) + epsilon)
    new_master = master - learning_rate * (update + weight_decay * master)
    return (new_master, new_first, new_second)

def restore(checkpoints, block_holder):
    merged = jnp.zeros((3, N_GRP, N_DP, BLOCKS, BLK), jnp.float32)
    for offset in (1, 2):
        rolled = jnp.roll(checkpoints[:, :, :, offset - 1], -offset, axis=1)
        is_held = block_holder == offset
        slot_index = jnp.clip(jnp.cumsum(is_held.astype(jnp.int32), axis=-1) - 1, 0, MOST - 1).astype(jnp.int32)
        slot_grid = jnp.broadcast_to(slot_index[None, :, :, :, None], (3, N_GRP, N_DP, BLOCKS, BLK))
        picked = jnp.take_along_axis(rolled, slot_grid, axis=3)
        merged = jnp.where(is_held[None, :, :, :, None], picked, merged)
    return merged.reshape(3, N_GRP, N_DP * ROWS_DEV, D)

def reference(master, first_moment, second_moment, gradient, checkpoints, block_holder, failed_member):
    restored = restore(checkpoints, block_holder)
    failed_rows = failed_member[None, :] == jnp.arange(N_GRP, dtype=jnp.int32)[:, None]
    failed_rows = jnp.repeat(failed_rows, ROWS_DEV, axis=1)[:, :, None]
    master_state = jnp.where(failed_rows, restored[0], master)
    first_state = jnp.where(failed_rows, restored[1], first_moment)
    second_state = jnp.where(failed_rows, restored[2], second_moment)
    new_master, new_first, new_second = adamw_step(master_state, first_state, second_state, gradient)
    return (new_master, new_first, new_second, new_master.astype(jnp.bfloat16))
```

```python
import functools

import jax
import jax.numpy as jnp
from jax import lax
from jax.experimental import pallas as pl
from jax.experimental.pallas import tpu as pltpu
from jax.sharding import PartitionSpec as P

MESH = pl.DeviceIdType.MESH
NX, NZ, NY = 4, 8, 4
STEPS = ((1, 0, 0), (-1, 0, 0), (0, 1, 0), (0, -1, 0), (0, 0, 1), (0, 0, -1))

TREE = (
    (0, 2, 3, 4, 5, 1, 0), (4, 0, 2, 1), (28, 3, 4, 0, 5), (96, 3, 1), (32,), (1, 2, 1, 4, 0), (3, 0, 1, 2),
    (36, 2), (8, 5, 2, 1), (100, 1), (24, 3, 5), (60, 3, 4), (5, 2, 1, 0), (64,), (124, 1, 3), (29, 3, 4),
    (31,), (33, 0), (7, 0, 1), (97, 3), (20, 0, 5, 1), (35, 5, 0, 3), (40, 2), (99, 3), (2, 2, 1), (11, 5, 2,
    0, 1), (56, 0, 4), (37,), (12, 2, 1), (104,), (120,), (65,), (9, 1, 2, 0), (68, 2), (61,), (27, 0, 5),
    (25, 3), (39,), (44, 4, 0, 5), (101, 1), (125, 1, 3), (52, 4, 3), (6, 0), (92,), (30, 0), (23, 3), (63,),
    (67, 2), (15, 1), (103,), (127, 3, 5, 1), (43,), (16,), (116, 3), (57,), (34, 0), (21, 4, 1), (88, 3, 5),
    (13, 2), (98, 2), (121,), (41,), (72, 5), (107,), (45, 4), (10, 2, 1, 0), (48,), (59, 3), (71,), (108,),
    (19, 1), (76, 5), (17,), (105, 2), (53, 3, 4), (26, 0), (123, 3), (38,), (69, 2), (102,), (112, 1), (62,
    0), (14, 2), (93, 3), (22, 1), (47,), (84,), (66, 2), (109, 2), (111,), (55, 3, 0), (42,), (73, 4, 2),
    (95,), (46, 0), (126, 3), (49, 0), (58,), (18, 0), (117,), (119,), (94, 3), (70,), (106, 2), (54, 0),
    (91,), (89, 3), (87,), (113, 4), (115, 1), (51,), (78, 2), (77,), (80,), (74,), (75,), (122,), (81,),
    (110,), (118,), (90,), (50,), (83,), (82,), (79,), (114,), (85,), (86,),
)

beta_one = 0.9
beta_two = 0.95
learning_rate = 0.05
weight_decay = 0.1
epsilon = 1e-08
correct_one = 1.0 - 0.9**10
correct_two = 1.0 - 0.95**10


def moved(cell, direction):
    x, z, y = cell // 32, cell // 4 % 8, cell % 4
    a, b, c = STEPS[direction]
    return ((x + a) % NX * 8 + (z + b) % NZ) * 4 + (y + c) % NY


def fold(rows):
    return jnp.concatenate([rows[:, 2048 * q : 2048 * q + 2048] for q in range(4)], axis=0)


def unfold(folded):
    return jnp.concatenate([folded[4 * q : 4 * q + 4] for q in range(4)], axis=1)


def adamw_step(master, first, second, grad_float):
    new_first = beta_one * first + (1.0 - beta_one) * grad_float
    new_second = beta_two * second + (1.0 - beta_two) * grad_float * grad_float
    update = new_first / correct_one / (jnp.sqrt(new_second / correct_two) + epsilon)
    new_master = master - learning_rate * (update + weight_decay * master)
    return (new_master, new_first, new_second)


def gather_kernel(
    holder_ref, failed_ref, ckpt_hbm, master_hbm, first_hbm, second_hbm, grad_hbm,
    gathered, master_out, first_out, second_out,
    ckpt, state, grad, send_a, send_b, recv_a, recv_b,
    load_sem, ex_send, ex_recv, ag_send, ag_recv,
):
    dp = lax.axis_index("dp")
    grp = lax.axis_index("grp")
    x, z, y = dp // 32, lax.rem(dp // 4, 8), lax.rem(dp, 4)

    def slot(dx, dz, dy):
        return (lax.rem(x + dx + NX, NX) * 8 + lax.rem(z + dz + NZ, NZ)) * 4 + lax.rem(y + dy + NY, NY)

    neighbours = [(slot(*step), grp) for step in STEPS]
    peers = [(dp, lax.rem(grp + k, 4)) for k in (1, 2, 3)]

    loads = [pltpu.make_async_copy(ckpt_hbm, ckpt, load_sem.at[0])]
    for i, ref in enumerate((master_hbm, first_hbm, second_hbm)):
        loads.append(pltpu.make_async_copy(ref, state.at[i], load_sem.at[i + 1]))
    loads.append(pltpu.make_async_copy(grad_hbm, grad, load_sem.at[4]))
    for load in loads:
        load.start()

    barrier = pltpu.get_barrier_semaphore()
    for device in neighbours + peers:
        pl.semaphore_signal(barrier, inc=1, device_id=device, device_id_type=MESH)

    loads[0].wait()
    for o in range(2):
        for k in range(3):
            head = ckpt[k, o, 0:8, :]
            tail = ckpt[k, o, 8:12, :]
            send_a[o, k] = jnp.concatenate([head[:, :1024], head[:, 1024:]], axis=0).astype(jnp.bfloat16)
            send_b[o, k] = jnp.concatenate(
                [tail[:, 512 * c : 512 * c + 512] for c in range(4)], axis=0
            ).astype(jnp.bfloat16)
    pl.semaphore_wait(barrier, len(neighbours) + len(peers))

    exchange = []
    for part, (src, dst) in enumerate(((send_a, recv_a), (send_b, recv_b))):
        for o in (1, 0):
            copy = pltpu.make_async_remote_copy(
                src_ref=src.at[o],
                dst_ref=dst.at[o],
                send_sem=ex_send.at[2 * part + o],
                recv_sem=ex_recv.at[2 * part + o],
                device_id=peers[2 - o],
                device_id_type=MESH,
            )
            copy.start()
            exchange.append(copy)

    rows = lax.broadcasted_iota(jnp.int32, (16, 32), 0)
    wanted = jnp.zeros((16, 32), jnp.int32)
    seen_near = jnp.int32(0)
    for b in range(16):
        near = holder_ref[0, b] == 1
        s = jnp.where(near, seen_near, b - seen_near)
        source = s + jnp.where(near, jnp.where(s < 8, 0, 8), jnp.where(s < 8, 8, 12))
        wanted = jnp.where(rows == 4 * (b % 4) + b // 4, source, wanted)
        seen_near = seen_near + jnp.where(near, 1, 0)
    lookup = jnp.where(lax.broadcasted_iota(jnp.int32, (16, 32), 1) == wanted, 1.0, 0.0).astype(jnp.bfloat16)
    failed = failed_ref[0] == grp

    for load in loads[1:]:
        load.wait()
    local = [fold(state[k]) for k in range(3)]
    grad_float = fold(grad[...].astype(jnp.float32))
    for copy in exchange:
        copy.wait_recv()
    chosen = []
    for k in range(3):
        parts = []
        for o in range(2):
            a = recv_a[o, k].astype(jnp.float32)
            parts.append(jnp.concatenate([a[:8], a[8:]], axis=1))
        tails = []
        for o in range(2):
            b = recv_b[o, k].astype(jnp.float32)
            tails.append(jnp.concatenate([b[4 * c : 4 * c + 4] for c in range(4)], axis=1))
        parts.append(jnp.concatenate(tails, axis=0))
        parts.append(jnp.zeros((8, 2048), jnp.float32))
        held = jnp.concatenate(parts, axis=0).astype(jnp.bfloat16)
        restored = jnp.dot(lookup, held, preferred_element_type=jnp.float32)
        chosen.append(jnp.where(failed, restored, local[k]))
    new_master, new_first, new_second = adamw_step(*chosen, grad_float)
    gathered[dp] = new_master.astype(jnp.bfloat16)

    def copy_of(cell, direction):
        there = moved(cell, direction)
        place = gathered.at[slot(-(cell // 32), -(cell // 4 % 8), -(cell % 4))]
        return pltpu.make_async_remote_copy(
            src_ref=place,
            dst_ref=place,
            send_sem=ag_send.at[there],
            recv_sem=ag_recv.at[there],
            device_id=neighbours[direction],
            device_id_type=MESH,
        )

    def arrival_of(cell):
        place = gathered.at[slot(-(cell // 32), -(cell // 4 % 8), -(cell % 4))]
        return pltpu.make_async_remote_copy(
            src_ref=place,
            dst_ref=place,
            send_sem=ag_send.at[cell],
            recv_sem=ag_recv.at[cell],
            device_id=neighbours[0],
            device_id_type=MESH,
        )

    sent = []
    for cell, *directions in TREE:
        if cell:
            arrival_of(cell).wait_recv()
        for direction in directions:
            copy = copy_of(cell, direction)
            copy.start()
            sent.append(copy)
        if not cell:
            master_out[...] = unfold(new_master)
            first_out[...] = unfold(new_first)
            second_out[...] = unfold(new_second)
            for copy in exchange:
                copy.wait_send()
    for copy in sent:
        copy.wait_send()


def place_kernel(gathered, master, first, second, weights, master_out, first_out, second_out, sem):
    step = pl.program_id(0)
    copies = [
        pltpu.make_async_copy(src, dst, sem.at[i])
        for i, (src, dst) in enumerate(((master, master_out), (first, first_out), (second, second_out)))
    ]

    @pl.when(step == 0)
    def _():
        for copy in copies:
            copy.start()

    for t in range(2):
        shards = [gathered[(2 * step + t) * 4 + k].astype(jnp.float32) for k in range(4)]
        for q in range(4):
            tile = jnp.concatenate([shard[4 * q : 4 * q + 4] for shard in shards], axis=0)
            weights[16 * t : 16 * t + 16, 2048 * q : 2048 * q + 2048] = tile.astype(jnp.bfloat16)

    @pl.when(step == pl.num_programs(0) - 1)
    def _():
        for copy in copies:
            copy.wait()


def per_device(master, first_moment, second_moment, gradient, checkpoints, block_holder, failed_member):
    rows = jax.ShapeDtypeStruct((4, 8192), jnp.float32)
    gathered, new_master, new_first, new_second = pl.pallas_call(
        gather_kernel,
        out_shape=[pltpu.VMEM((128, 16, 2048), jnp.bfloat16)] + [pltpu.VMEM((4, 8192), jnp.float32)] * 3,
        in_specs=[pl.BlockSpec(memory_space=pltpu.SMEM)] * 2 + [pl.BlockSpec(memory_space=pl.ANY)] * 5,
        out_specs=[pl.BlockSpec(memory_space=pltpu.VMEM)] * 4,
        scratch_shapes=[
            pltpu.VMEM((3, 2, 12, 2048), jnp.float32),
            pltpu.VMEM((3, 4, 8192), jnp.float32),
            pltpu.VMEM((4, 8192), jnp.bfloat16),
            pltpu.VMEM((2, 3, 16, 1024), jnp.bfloat16),
            pltpu.VMEM((2, 3, 16, 512), jnp.bfloat16),
            pltpu.VMEM((2, 3, 16, 1024), jnp.bfloat16),
            pltpu.VMEM((2, 3, 16, 512), jnp.bfloat16),
            pltpu.SemaphoreType.DMA((5,)),
            pltpu.SemaphoreType.DMA((4,)),
            pltpu.SemaphoreType.DMA((4,)),
            pltpu.SemaphoreType.DMA((128,)),
            pltpu.SemaphoreType.DMA((128,)),
        ],
        compiler_params=pltpu.CompilerParams(
            collective_id=0, has_side_effects=True, vmem_limit_bytes=40 * 2**20
        ),
        name="restore_step_gather",
    )(
        block_holder.reshape(1, 16), failed_member, checkpoints.reshape(3, 2, 12, 2048), master.reshape(4, 8192),
        first_moment.reshape(4, 8192), second_moment.reshape(4, 8192), gradient.reshape(4, 8192),
    )
    weights, new_master, new_first, new_second = pl.pallas_call(
        place_kernel,
        grid=(16,),
        out_shape=[jax.ShapeDtypeStruct((512, 8192), jnp.bfloat16), rows, rows, rows],
        in_specs=[pl.BlockSpec(memory_space=pltpu.VMEM)] * 4,
        out_specs=[pl.BlockSpec((16 * 2, 8192), lambda i: (i, 0))] + [pl.BlockSpec(memory_space=pl.ANY)] * 3,
        scratch_shapes=[pltpu.SemaphoreType.DMA((3,))],
        compiler_params=pltpu.CompilerParams(vmem_limit_bytes=40 * 2**20),
        name="place_rows",
    )(gathered, new_master, new_first, new_second)
    whole = (1, 4, 8192)
    return (
        new_master.reshape(whole), new_first.reshape(whole), new_second.reshape(whole), weights.reshape(1, 512, 8192)
    )


def solution(mesh):
    return jax.shard_map(
        per_device,
        mesh=mesh,
        in_specs=(
            P("grp", "dp", None),
            P("grp", "dp", None),
            P("grp", "dp", None),
            P("grp", "dp", None),
            P(None, "grp", "dp", None, None, None),
            P("grp", "dp", None),
            P("dp"),
        ),
        out_specs=(
            P("grp", "dp", None),
            P("grp", "dp", None),
            P("grp", "dp", None),
            P("grp", None, None),
        ),
        check_vma=False,
    )
```

```python
import functools

import jax
import jax.numpy as jnp
from jax import lax
from jax.experimental import pallas as pl
from jax.experimental.pallas import tpu as pltpu
from jax.sharding import PartitionSpec as P

MESH = pl.DeviceIdType.MESH
NX, NZ, NY = 4, 8, 4
STEPS = ((1, 0, 0), (-1, 0, 0), (0, 1, 0), (0, -1, 0), (0, 0, 1), (0, 0, -1))

TREE = (
    (0, 2, 3, 4, 5, 1, 0), (4, 0, 2, 1), (28, 3, 4, 0, 5), (96, 3, 1), (32,), (1, 2, 1, 4, 0), (3, 0, 1, 2),
    (36, 2), (8, 5, 2, 1), (100, 1), (24, 3, 5), (60, 3, 4), (5, 2, 1, 0), (64,), (124, 1, 3), (29, 3, 4),
    (31,), (33, 0), (7, 0, 1), (97, 3), (20, 0, 5, 1), (35, 5, 0, 3), (40, 2), (99, 3), (2, 2, 1), (11, 5, 2,
    0, 1), (56, 0, 4), (37,), (12, 2, 1), (104,), (120,), (65,), (9, 1, 2, 0), (68, 2), (61,), (27, 0, 5),
    (25, 3), (39,), (44, 4, 0, 5), (101, 1), (125, 1, 3), (52, 4, 3), (6, 0), (92,), (30, 0), (23, 3), (63,),
    (67, 2), (15, 1), (103,), (127, 3, 5, 1), (43,), (16,), (116, 3), (57,), (34, 0), (21, 4, 1), (88, 3, 5),
    (13, 2), (98, 2), (121,), (41,), (72, 5), (107,), (45, 4), (10, 2, 1, 0), (48,), (59, 3), (71,), (108,),
    (19, 1), (76, 5), (17,), (105, 2), (53, 3, 4), (26, 0), (123, 3), (38,), (69, 2), (102,), (112, 1), (62,
    0), (14, 2), (93, 3), (22, 1), (47,), (84,), (66, 2), (109, 2), (111,), (55, 3, 0), (42,), (73, 4, 2),
    (95,), (46, 0), (126, 3), (49, 0), (58,), (18, 0), (117,), (119,), (94, 3), (70,), (106, 2), (54, 0),
    (91,), (89, 3), (87,), (113, 4), (115, 1), (51,), (78, 2), (77,), (80,), (74,), (75,), (122,), (81,),
    (110,), (118,), (90,), (50,), (83,), (82,), (79,), (114,), (85,), (86,),
)

beta_one = 0.9
beta_two = 0.95
learning_rate = 0.05
weight_decay = 0.1
epsilon = 1e-08
correct_one = 1.0 - 0.9**10
correct_two = 1.0 - 0.95**10


def moved(cell, direction):
    x, z, y = cell // 32, cell // 4 % 8, cell % 4
    a, b, c = STEPS[direction]
    return ((x + a) % NX * 8 + (z + b) % NZ) * 4 + (y + c) % NY


def adamw_step(master, first, second, grad_float):
    new_first = beta_one * first + (1.0 - beta_one) * grad_float
    new_second = beta_two * second + (1.0 - beta_two) * grad_float * grad_float
    update = new_first / correct_one / (jnp.sqrt(new_second / correct_two) + epsilon)
    new_master = master - learning_rate * (update + weight_decay * master)
    return (new_master, new_first, new_second)


def gather_kernel(
    failed_at, holder_hbm, ckpt_hbm, master_hbm, first_hbm, second_hbm, grad_hbm,
    weights, master_out, first_out, second_out,
    gathered, ckpt, state, grad, restored, send, recv, holder,
    load_sem, ex_send, ex_recv, ag_send, ag_recv,
):
    dp = lax.axis_index("dp")
    grp = lax.axis_index("grp")
    x, z, y = dp // 32, lax.rem(dp // 4, 8), lax.rem(dp, 4)

    def line(dx, dz):
        return lax.rem(x + dx + NX, NX) * 8 + lax.rem(z + dz + NZ, NZ)

    def slot(dx, dz, dy):
        return line(dx, dz) * 4 + lax.rem(y + dy + NY, NY)

    neighbours = [(slot(*step), grp) for step in STEPS]
    peers = [(dp, lax.rem(grp + k, 4)) for k in (1, 2, 3)]

    loads = [
        pltpu.make_async_copy(src, dst, load_sem.at[i])
        for i, (src, dst) in enumerate(
            (
                (ckpt_hbm, ckpt), (master_hbm, state.at[0]), (first_hbm, state.at[1]), (second_hbm, state.at[2]),
                (grad_hbm, grad), (holder_hbm, holder),
            )
        )
    ]
    for load in loads:
        load.start()

    barrier = pltpu.get_barrier_semaphore()
    for device in neighbours + peers:
        pl.semaphore_signal(barrier, inc=1, device_id=device, device_id_type=MESH)

    loads[0].wait()
    for s in range(12):
        for k in range(3):
            for o in range(2):
                send[o, s, k] = ckpt[k, s, pl.ds(o, 16, stride=2), :].astype(jnp.bfloat16)
    pl.semaphore_wait(barrier, len(neighbours) + len(peers))

    exchange = []
    for part in range(1):
        slots = pl.ds(part * 12, 12)
        for o in (1, 0):
            copy = pltpu.make_async_remote_copy(
                src_ref=send.at[o, slots],
                dst_ref=recv.at[o, slots],
                send_sem=ex_send.at[2 * part + o],
                recv_sem=ex_recv.at[2 * part + o],
                device_id=peers[2 - o],
                device_id_type=MESH,
            )
            copy.start()
            exchange.append(copy)
    for load in loads[1:]:
        load.wait()

    places = []
    seen_near = jnp.int32(0)
    for b in range(16):
        near = holder[0, b] == 1
        places.append((jnp.where(near, 0, 1), jnp.minimum(jnp.where(near, seen_near, b - seen_near), 11)))
        seen_near = seen_near + jnp.where(near, 1, 0)
    failed = failed_at[0] == grp
    for copy in exchange:
        copy.wait_recv()
    for b, (o, s) in enumerate(places):
        for k in range(3):
            restored[k, pl.ds(64 * (b % 4) + b // 4, 16, stride=4), :] = recv[o, s, k].astype(jnp.float32)
    chosen = [jnp.where(failed, restored[k], state[k]) for k in range(3)]
    new_master, new_first, new_second = adamw_step(*chosen, grad[...].astype(jnp.float32))
    gathered[dp] = new_master.astype(jnp.bfloat16)

    def copy_of(cell, direction):
        there = moved(cell, direction)
        place = gathered.at[slot(-(cell // 32), -(cell // 4 % 8), -(cell % 4))]
        return pltpu.make_async_remote_copy(
            src_ref=place,
            dst_ref=place,
            send_sem=ag_send.at[there],
            recv_sem=ag_recv.at[there],
            device_id=neighbours[direction],
            device_id_type=MESH,
        )

    def arrival_of(cell):
        place = gathered.at[slot(-(cell // 32), -(cell // 4 % 8), -(cell % 4))]
        return pltpu.make_async_remote_copy(
            src_ref=place,
            dst_ref=place,
            send_sem=ag_send.at[cell],
            recv_sem=ag_recv.at[cell],
            device_id=neighbours[0],
            device_id_type=MESH,
        )

    def place_rows(dx, dz):
        t = line(-dx, -dz)

        def columns(j, carry):
            for i in range(4):
                at = pl.multiple_of((4 * j + i) * 16, 16)
                shards = [gathered[4 * t + k, pl.ds(at, 16), :].astype(jnp.float32) for k in range(4)]
                for c in range(4):
                    tile = jnp.concatenate([shard[4 * c : 4 * c + 4] for shard in shards], axis=0)
                    lanes = pl.multiple_of((4 * j + i) * 512 + 128 * c, 128)
                    weights[pl.ds(pl.multiple_of(16 * t, 16), 16), pl.ds(lanes, 128)] = tile.astype(jnp.bfloat16)
            return carry

        lax.fori_loop(0, 16 // 4, columns, 0)

    sent = []
    arrived = [0] * 32
    ready = []
    for cell, *directions in TREE:
        if cell:
            arrival_of(cell).wait_recv()
        for direction in directions:
            copy = copy_of(cell, direction)
            copy.start()
            sent.append(copy)
        if not cell:
            master_out[...] = new_master
            first_out[...] = new_first
            second_out[...] = new_second
            for copy in exchange:
                copy.wait_send()
        arrived[cell // 4] += 1
        if arrived[cell // 4] == 4:
            ready.append(cell // 4)
        if ready:
            done = ready.pop(0)
            place_rows(done // 8, done % 8)
    for done in ready:
        place_rows(done // 8, done % 8)
    for copy in sent:
        copy.wait_send()


def output_kernel(*refs):
    copies = [pltpu.make_async_copy(refs[i], refs[i + 4], refs[8].at[i]) for i in range(3)]
    for i in range(8):
        rows = pl.ds(512 // 8 * i, 512 // 8)
        copies.append(pltpu.make_async_copy(refs[3].at[rows], refs[7].at[rows], refs[8].at[3 + i]))
    for copy in copies:
        copy.start()
    for copy in copies:
        copy.wait()


def tiles(rows):
    return rows.reshape(4, 64, 128).transpose(1, 0, 2).reshape(256, 128)


def rows_of(tiled):
    return tiled.reshape(64, 4, 128).transpose(1, 0, 2).reshape(1, 4, 8192)


def per_device(master, first_moment, second_moment, gradient, checkpoints, block_holder, failed_member):
    held = checkpoints.reshape(3, 2, 12, 16, 128).transpose(0, 2, 3, 1, 4).reshape(3, 12, 32, 128)
    operands = [block_holder.reshape(1, 16), held]
    operands += [tiles(value) for value in (master, first_moment, second_moment, gradient)]
    operands = [pltpu.with_memory_space_constraint(value, pltpu.HBM) for value in operands]
    shard = ((256, 128), jnp.float32)
    weights, new_master, new_first, new_second = pl.pallas_call(
        gather_kernel,
        out_shape=[pltpu.VMEM((512, 8192), jnp.bfloat16)] + [pltpu.VMEM(*shard)] * 3,
        in_specs=[pl.BlockSpec(memory_space=pltpu.SMEM)] + [pl.BlockSpec(memory_space=pltpu.HBM)] * 6,
        out_specs=[pl.BlockSpec(memory_space=pltpu.VMEM)] * 4,
        scratch_shapes=[
            pltpu.VMEM((128, 256, 128), jnp.bfloat16),
            pltpu.VMEM((3, 12, 32, 128), jnp.float32),
            pltpu.VMEM((3, 256, 128), jnp.float32),
            pltpu.VMEM((256, 128), jnp.bfloat16),
            pltpu.VMEM((3, 256, 128), jnp.float32),
            pltpu.VMEM((2, 12, 3, 16, 128), jnp.bfloat16),
            pltpu.VMEM((2, 12, 3, 16, 128), jnp.bfloat16),
            pltpu.SMEM((1, 16), jnp.int32),
            pltpu.SemaphoreType.DMA((6,)),
            pltpu.SemaphoreType.DMA((2 * 1,)),
            pltpu.SemaphoreType.DMA((2 * 1,)),
            pltpu.SemaphoreType.DMA((128,)),
            pltpu.SemaphoreType.DMA((128,)),
        ],
        compiler_params=pltpu.CompilerParams(
            collective_id=0, has_side_effects=True, vmem_limit_bytes=24 * 2**20
        ),
        name="restore_step_gather",
    )(failed_member, *operands)
    results = [
        pltpu.with_memory_space_constraint(value, pltpu.VMEM) for value in (new_master, new_first, new_second, weights)
    ]
    new_master, new_first, new_second, weights = pl.pallas_call(
        output_kernel,
        out_shape=[jax.ShapeDtypeStruct(*shard)] * 3 + [jax.ShapeDtypeStruct((512, 8192), jnp.bfloat16)],
        in_specs=[pl.BlockSpec(memory_space=pltpu.VMEM)] * 4,
        out_specs=[pl.BlockSpec(memory_space=pl.ANY)] * 4,
        scratch_shapes=[pltpu.SemaphoreType.DMA((3 + 8,))],
        compiler_params=pltpu.CompilerParams(vmem_limit_bytes=4 * 2**20),
        name="write_outputs",
    )(*results)
    return (rows_of(new_master), rows_of(new_first), rows_of(new_second), weights.reshape(1, 512, 8192))


def solution(mesh):
    return jax.shard_map(
        per_device,
        mesh=mesh,
        in_specs=(
            P("grp", "dp", None),
            P("grp", "dp", None),
            P("grp", "dp", None),
            P("grp", "dp", None),
            P(None, "grp", "dp", None, None, None),
            P("grp", "dp", None),
            P("dp"),
        ),
        out_specs=(
            P("grp", "dp", None),
            P("grp", "dp", None),
            P("grp", "dp", None),
            P("grp", None, None),
        ),
        check_vma=False,
    )
```

```python
import functools

import jax
import jax.numpy as jnp
from jax import lax
from jax.experimental import pallas as pl
from jax.experimental.pallas import tpu as pltpu
from jax.sharding import PartitionSpec as P

MESH = pl.DeviceIdType.MESH
NX, NZ, NY = 4, 8, 4
PARTS = 3
STEPS = ((1, 0, 0), (-1, 0, 0), (0, 1, 0), (0, -1, 0), (0, 0, 1), (0, 0, -1))

TREE = (
    (0, 0, 5, 4, 3, 2, 1, 0), (0, 28, 3, 0, 1), (0, 4, 2, 1, 0), (0, 96, 1, 5), (0, 32, 4), (0, 3, 2, 5, 3,
    0), (0, 1, 3, 2, 1), (0, 24, 3, 0), (0, 60, 0, 4, 5), (0, 124, 3), (0, 8, 4, 0, 2), (0, 36), (0, 100, 2),
    (0, 7, 1, 2, 0), (0, 31, 1, 3, 5), (0, 99), (0, 33), (0, 35, 0), (0, 64, 2, 4), (0, 5, 0), (0, 29, 1, 3),
    (0, 56, 5), (0, 97, 2), (0, 12, 1), (0, 20, 0, 1, 3), (0, 2, 2, 0, 1), (0, 92, 3), (0, 103, 2, 5), (0,
    61), (0, 104), (0, 120), (0, 40, 2), (0, 127, 1, 3), (0, 11, 2, 0), (0, 27, 3), (0, 39, 0), (0, 125, 4,
    1), (0, 63), (0, 9, 2, 1), (0, 68, 2), (0, 25, 0, 3, 1, 4), (0, 67), (0, 108), (0, 101, 1), (0, 16), (0,
    37, 2), (0, 116, 3, 4), (0, 6, 2, 0), (0, 30), (0, 88), (0, 65), (0, 52, 3, 0), (0, 98), (0, 107, 5), (0,
    123, 1), (0, 34, 3, 0), (0, 95, 5), (0, 44, 4, 0), (0, 23, 3, 1), (0, 59, 3), (0, 126, 3), (0, 43, 2, 0),
    (0, 93), (0, 15, 1), (0, 21, 4), (0, 71), (0, 105), (0, 13, 2, 1), (0, 112), (0, 102), (0, 26), (0, 57,
    3), (0, 121, 1), (0, 72), (0, 48, 0), (0, 38, 0), (0, 69), (0, 41, 0), (0, 62, 3), (0, 106, 2), (0, 84,
    5), (0, 91), (0, 117), (0, 10, 2, 0), (0, 19), (0, 66), (0, 119), (0, 47, 0), (0, 55, 3), (0, 76), (0,
    111, 2), (0, 94), (0, 45), (0, 17, 1), (0, 122, 1, 3), (0, 75, 5), (0, 109), (0, 110, 2, 1), (0, 53, 3,
    0), (0, 80, 4), (0, 89), (0, 14, 2), (0, 87), (0, 58, 3), (0, 22), (0, 70), (0, 113), (0, 115, 1), (0, 51,
    5), (0, 73, 2), (0, 90, 3), (0, 114, 1), (0, 118), (0, 74), (0, 42, 2), (0, 78), (0, 18), (0, 49), (0,
    81), (0, 79), (0, 83), (0, 54), (0, 77), (0, 85), (0, 82), (0, 50), (0, 86), (0, 46),
)

beta_one = 0.9
beta_two = 0.95
learning_rate = 0.05
weight_decay = 0.1
epsilon = 1e-08
correct_one = 1.0 - 0.9**10
correct_two = 1.0 - 0.95**10


def moved(cell, direction):
    x, z, y = cell // 32, cell // 4 % 8, cell % 4
    a, b, c = STEPS[direction]
    return ((x + a) % NX * 8 + (z + b) % NZ) * 4 + (y + c) % NY


def adamw_step(master, first, second, grad_float):
    new_first = beta_one * first + (1.0 - beta_one) * grad_float
    new_second = beta_two * second + (1.0 - beta_two) * grad_float * grad_float
    update = new_first / correct_one / (jnp.sqrt(new_second / correct_two) + epsilon)
    new_master = master - learning_rate * (update + weight_decay * master)
    return (new_master, new_first, new_second)


def gather_kernel(
    failed_at, holder_hbm, ckpt_hbm, master_hbm, first_hbm, second_hbm, grad_hbm,
    weights, master_out, first_out, second_out,
    gathered, ckpt, state, grad, restored, send, recv, holder,
    load_sem, ex_send, ex_recv, ag_send, ag_recv,
):
    dp = lax.axis_index("dp")
    grp = lax.axis_index("grp")
    x, z, y = dp // 32, lax.rem(dp // 4, 8), lax.rem(dp, 4)

    x_at = [lax.rem(x - d + NX, NX) * 32 for d in range(NX)]
    z_at = [lax.rem(z - d + NZ, NZ) * 4 for d in range(NZ)]
    y_at = [lax.rem(y - d + NY, NY) for d in range(NY)]
    shard_at = [x_at[cell // 32] + z_at[cell // 4 % 8] + y_at[cell % 4] for cell in range(128)]
    neighbours = [(shard_at[(-a % NX * 8 + -b % NZ) * 4 + -c % NY], grp) for a, b, c in STEPS]
    peers = [(dp, lax.rem(grp + k, 4)) for k in (1, 2, 3)]

    loads = [
        pltpu.make_async_copy(src, dst, load_sem.at[i])
        for i, (src, dst) in enumerate(
            (
                *((ckpt_hbm.at[:, pl.ds(4 * p, 4)], ckpt.at[:, pl.ds(4 * p, 4)]) for p in range(PARTS)),
                (master_hbm, state.at[0]), (first_hbm, state.at[1]), (second_hbm, state.at[2]),
                (grad_hbm, grad), (holder_hbm, holder),
            )
        )
    ]
    for load in loads:
        load.start()

    barrier = pltpu.get_barrier_semaphore()
    for device in neighbours + peers:
        pl.semaphore_signal(barrier, inc=1, device_id=device, device_id_type=MESH)

    odd = lax.rem(grp, 2) == 1
    sends_near = jnp.logical_or(odd, failed_at[0] == lax.rem(grp + 3, 4))

    def part_copy(src, o, part, kind, device):
        return pltpu.make_async_remote_copy(
            src_ref=src.at[pl.ds(4 * part, 4)],
            dst_ref=recv.at[o, pl.ds(4 * part, 4)],
            send_sem=ex_send.at[PARTS * kind + part],
            recv_sem=ex_recv.at[PARTS * o + part],
            device_id=device,
            device_id_type=MESH,
        )

    first_copies = [part_copy(send.at[0], 0, part, 0, peers[2]) for part in range(PARTS)]
    far_copies = [part_copy(send.at[1], 1, part, 1, peers[1]) for part in range(PARTS)]
    onward_copies = [part_copy(recv.at[0], 1, part, 2, peers[2]) for part in range(PARTS)]
    for part in range(PARTS):
        loads[part].wait()
        for s in range(4 * part, 4 * part + 4):
            for k in range(3):
                near = ckpt[k, s, pl.ds(0, 16, stride=2), :].astype(jnp.bfloat16)
                far = ckpt[k, s, pl.ds(1, 16, stride=2), :].astype(jnp.bfloat16)
                send[0, s, k] = jnp.where(sends_near, near, far)
                send[1, s, k] = far
        if part == 0:
            pl.semaphore_wait(barrier, len(neighbours) + len(peers))
        first_copies[part].start()
        pl.when(odd)(far_copies[part].start)
    for load in loads[PARTS:]:
        load.wait()

    places = []
    seen_near = jnp.int32(0)
    for b in range(16):
        near = holder[0, b] == 1
        places.append((jnp.where(near, 0, 1), jnp.minimum(jnp.where(near, seen_near, b - seen_near), 11)))
        seen_near = seen_near + jnp.where(near, 1, 0)
    failed = failed_at[0] == grp
    for part in range(PARTS):
        first_copies[part].wait_recv()
        pl.when(odd)(onward_copies[part].start)
    for copy in far_copies:
        copy.wait_recv()
    for b, (o, s) in enumerate(places):
        for k in range(3):
            restored[k, pl.ds(64 * (b % 4) + b // 4, 16, stride=4), :] = recv[o, s, k].astype(jnp.float32)
    chosen = [jnp.where(failed, restored[k], state[k]) for k in range(3)]
    new_master, new_first, new_second = adamw_step(*chosen, grad[...].astype(jnp.float32))
    gathered[dp] = new_master.astype(jnp.bfloat16)

    def shard_copy(cell, arrives, direction):
        place = gathered.at[shard_at[cell]]
        return pltpu.make_async_remote_copy(
            src_ref=place,
            dst_ref=place,
            send_sem=ag_send,
            recv_sem=ag_recv.at[arrives],
            device_id=neighbours[direction],
            device_id_type=MESH,
        )

    def place_rows(t):

        for j in range(16):
            shards = [gathered[4 * t + k, 16 * j : 16 * j + 16, :].astype(jnp.float32) for k in range(4)]
            for c in range(4):
                tile = jnp.concatenate([shard[4 * c : 4 * c + 4] for shard in shards], axis=0)
                lanes = 512 * j + 128 * c
                weights[pl.ds(pl.multiple_of(16 * t, 16), 16), lanes : lanes + 128] = tile.astype(jnp.bfloat16)

    def place_lot(low, count):
        def place(i, carry):
            place_rows(i // count * 8 + lax.rem(z + i % count + low, NZ))
            return carry

        lax.fori_loop(0, NX * count, place, 0)

    def in_lot(cell, low, count):
        return (-(cell // 4 % 8) - low) % NZ < count

    lots = [(6, 5), (5, 1), (3, 1), (4, 1)]
    started = max(i for i, (_, _, *directions) in enumerate(TREE) if directions)
    started = max(started, max(i for i, (_, cell, *_) in enumerate(TREE) if in_lot(cell, *lots[0])))
    for _, cell, *directions in TREE[: started + 1]:
        if cell:
            shard_copy(cell, cell, 0).wait_recv()
        for direction in directions:
            shard_copy(cell, moved(cell, direction), direction).start()
        if not cell:
            master_out[...] = new_master
            first_out[...] = new_first
            second_out[...] = new_second
            for copy in first_copies:
                copy.wait_send()

            @pl.when(odd)
            def _():
                for copy in far_copies + onward_copies:
                    copy.wait_send()
    place_lot(*lots[0])
    for lot in lots[1:]:
        for _, cell in TREE[started + 1 :]:
            if in_lot(cell, *lot):
                shard_copy(cell, cell, 0).wait_recv()
        place_lot(*lot)
    everything = gathered.at[pl.ds(0, 127)]
    pltpu.make_async_remote_copy(
        src_ref=everything, dst_ref=everything, send_sem=ag_send, recv_sem=ag_recv.at[0],
        device_id=neighbours[0], device_id_type=MESH,
    ).wait_send()


def output_kernel(*refs):
    copies = [pltpu.make_async_copy(refs[i], refs[i + 4], refs[8].at[i]) for i in range(3)]
    for i in range(8):
        rows = pl.ds(512 // 8 * i, 512 // 8)
        copies.append(pltpu.make_async_copy(refs[3].at[rows], refs[7].at[rows], refs[8].at[3 + i]))
    for copy in copies:
        copy.start()
    for copy in copies:
        copy.wait()


def tiles(rows):
    return rows.reshape(4, 64, 128).transpose(1, 0, 2).reshape(256, 128)


def rows_of(tiled):
    return tiled.reshape(64, 4, 128).transpose(1, 0, 2).reshape(1, 4, 8192)


def per_device(master, first_moment, second_moment, gradient, checkpoints, block_holder, failed_member):
    held = checkpoints.reshape(3, 2, 12, 16, 128).transpose(0, 2, 3, 1, 4).reshape(3, 12, 32, 128)
    operands = [block_holder.reshape(1, 16), held]
    operands += [tiles(value) for value in (master, first_moment, second_moment, gradient)]
    operands = [pltpu.with_memory_space_constraint(value, pltpu.HBM) for value in operands]
    shard = ((256, 128), jnp.float32)
    weights, new_master, new_first, new_second = pl.pallas_call(
        gather_kernel,
        out_shape=[pltpu.VMEM((512, 8192), jnp.bfloat16)] + [pltpu.VMEM(*shard)] * 3,
        in_specs=[pl.BlockSpec(memory_space=pltpu.SMEM)] + [pl.BlockSpec(memory_space=pltpu.HBM)] * 6,
        out_specs=[pl.BlockSpec(memory_space=pltpu.VMEM)] * 4,
        scratch_shapes=[
            pltpu.VMEM((128, 256, 128), jnp.bfloat16),
            pltpu.VMEM((3, 12, 32, 128), jnp.float32),
            pltpu.VMEM((3, 256, 128), jnp.float32),
            pltpu.VMEM((256, 128), jnp.bfloat16),
            pltpu.VMEM((3, 256, 128), jnp.float32),
            pltpu.VMEM((2, 12, 3, 16, 128), jnp.bfloat16),
            pltpu.VMEM((2, 12, 3, 16, 128), jnp.bfloat16),
            pltpu.SMEM((1, 16), jnp.int32),
            pltpu.SemaphoreType.DMA((PARTS + 5,)),
            pltpu.SemaphoreType.DMA((3 * PARTS,)),
            pltpu.SemaphoreType.DMA((2 * PARTS,)),
            pltpu.SemaphoreType.DMA,
            pltpu.SemaphoreType.DMA((128,)),
        ],
        compiler_params=pltpu.CompilerParams(
            collective_id=0, has_side_effects=True, vmem_limit_bytes=24 * 2**20
        ),
        name="restore_step_gather",
    )(failed_member, *operands)
    results = [
        pltpu.with_memory_space_constraint(value, pltpu.VMEM) for value in (new_master, new_first, new_second, weights)
    ]
    new_master, new_first, new_second, weights = pl.pallas_call(
        output_kernel,
        out_shape=[jax.ShapeDtypeStruct(*shard)] * 3 + [jax.ShapeDtypeStruct((512, 8192), jnp.bfloat16)],
        in_specs=[pl.BlockSpec(memory_space=pltpu.VMEM)] * 4,
        out_specs=[pl.BlockSpec(memory_space=pl.ANY)] * 4,
        scratch_shapes=[pltpu.SemaphoreType.DMA((3 + 8,))],
        compiler_params=pltpu.CompilerParams(vmem_limit_bytes=4 * 2**20),
        name="write_outputs",
    )(*results)
    return (rows_of(new_master), rows_of(new_first), rows_of(new_second), weights.reshape(1, 512, 8192))


def solution(mesh):
    return jax.shard_map(
        per_device,
        mesh=mesh,
        in_specs=(
            P("grp", "dp", None),
            P("grp", "dp", None),
            P("grp", "dp", None),
            P("grp", "dp", None),
            P(None, "grp", "dp", None, None, None),
            P("grp", "dp", None),
            P("dp"),
        ),
        out_specs=(
            P("grp", "dp", None),
            P("grp", "dp", None),
            P("grp", "dp", None),
            P("grp", None, None),
        ),
        check_vma=False,
    )
```

```python
import functools

import jax
import jax.numpy as jnp
from jax import lax
from jax.experimental import pallas as pl
from jax.experimental.pallas import tpu as pltpu
from jax.sharding import PartitionSpec as P

MESH = pl.DeviceIdType.MESH
NX, NZ, NY = 4, 8, 4
PARTS = 3
STEPS = ((1, 0, 0), (-1, 0, 0), (0, 1, 0), (0, -1, 0), (0, 0, 1), (0, 0, -1))

TREE = (
    (0, 0, 5, 4, 3, 2, 1, 0), (0, 28, 3, 0, 1), (0, 4, 2, 1, 0), (0, 96, 1, 5), (0, 32, 4), (0, 3, 2, 5, 3,
    0), (0, 1, 3, 2, 1), (0, 24, 3, 0), (0, 60, 0, 4, 5), (0, 124, 3), (0, 8, 4, 0, 2), (0, 36), (0, 100, 2),
    (0, 7, 1, 2, 0), (0, 31, 1, 3, 5), (0, 99), (0, 33), (0, 35, 0), (0, 64, 2, 4), (0, 5, 0), (0, 29, 1, 3),
    (0, 56, 5), (0, 97, 2), (0, 20, 0, 1, 3), (0, 12, 1), (0, 2, 2, 0, 1), (0, 92, 3), (0, 103, 2, 5), (0,
    120), (0, 104), (0, 61), (0, 40, 2), (0, 127, 1, 3), (0, 27, 3), (0, 11, 2, 0), (0, 39, 0), (0, 63), (0,
    125, 4, 1), (0, 25, 0, 3, 1, 4), (0, 68, 2), (0, 9, 2, 1), (0, 67), (0, 116, 3, 4), (0, 16), (0, 101, 1),
    (0, 37, 2), (0, 108), (0, 30), (0, 88), (0, 6, 2, 0), (0, 65), (0, 52, 3, 0), (0, 98), (0, 123, 1), (0,
    107, 5), (0, 34, 3, 0), (0, 95, 5), (0, 23, 3, 1), (0, 44, 4, 0), (0, 59, 3), (0, 43, 2, 0), (0, 126, 3),
    (0, 93), (0, 21, 4), (0, 15, 1), (0, 71), (0, 121, 1), (0, 112), (0, 72), (0, 102), (0, 57, 3), (0, 105),
    (0, 26), (0, 48, 0), (0, 13, 2, 1), (0, 38, 0), (0, 69), (0, 62, 3), (0, 41, 0), (0, 106, 2), (0, 84, 5),
    (0, 91), (0, 19), (0, 10, 2, 0), (0, 117), (0, 66), (0, 119), (0, 55, 3), (0, 47, 0), (0, 76), (0, 94),
    (0, 111, 2), (0, 122, 1, 3), (0, 17, 1), (0, 45), (0, 75, 5), (0, 89), (0, 53, 3, 0), (0, 110, 2, 1), (0,
    80, 4), (0, 109), (0, 58, 3), (0, 14, 2), (0, 87), (0, 22), (0, 70), (0, 90, 3), (0, 51, 5), (0, 115, 1),
    (0, 73, 2), (0, 113), (0, 118), (0, 114, 1), (0, 42, 2), (0, 78), (0, 49), (0, 74), (0, 18), (0, 79), (0,
    54), (0, 81), (0, 83), (0, 77), (0, 85), (0, 86), (0, 82), (0, 50), (0, 46),
)

beta_one = 0.9
beta_two = 0.95
learning_rate = 0.05
weight_decay = 0.1
epsilon = 1e-08
correct_one = 1.0 - 0.9**10
correct_two = 1.0 - 0.95**10


def moved(cell, direction):
    x, z, y = cell // 32, cell // 4 % 8, cell % 4
    a, b, c = STEPS[direction]
    return ((x + a) % NX * 8 + (z + b) % NZ) * 4 + (y + c) % NY


def adamw_step(master, first, second, grad_float):
    new_first = beta_one * first + (1.0 - beta_one) * grad_float
    new_second = beta_two * second + (1.0 - beta_two) * grad_float * grad_float
    update = new_first * (1.0 / correct_one) / (jnp.sqrt(new_second * (1.0 / correct_two)) + epsilon)
    new_master = master - learning_rate * (update + weight_decay * master)
    return (new_master, new_first, new_second)


def gather_kernel(
    failed_at, holder_hbm, ckpt_hbm, master_hbm, first_hbm, second_hbm, grad_hbm,
    weights, master_out, first_out, second_out,
    gathered, ckpt, state, grad, restored, send, recv, holder,
    load_sem, ex_send, ex_recv, ag_send, ag_recv,
):
    dp = lax.axis_index("dp")
    grp = lax.axis_index("grp")
    x, z, y = dp // 32, lax.rem(dp // 4, 8), lax.rem(dp, 4)

    x_at = [lax.rem(x - d + NX, NX) * 32 for d in range(NX)]
    z_at = [lax.rem(z - d + NZ, NZ) * 4 for d in range(NZ)]
    y_at = [lax.rem(y - d + NY, NY) for d in range(NY)]
    shard_at = [x_at[cell // 32] + z_at[cell // 4 % 8] + y_at[cell % 4] for cell in range(128)]
    neighbours = [(shard_at[(-a % NX * 8 + -b % NZ) * 4 + -c % NY], grp) for a, b, c in STEPS]
    peers = [(dp, lax.rem(grp + k, 4)) for k in (1, 2, 3)]

    loads = [
        pltpu.make_async_copy(src, dst, load_sem.at[i])
        for i, (src, dst) in enumerate(
            (
                *((ckpt_hbm.at[:, pl.ds(4 * p, 4)], ckpt.at[:, pl.ds(4 * p, 4)]) for p in range(PARTS)),
                (master_hbm, state.at[0]), (first_hbm, state.at[1]), (second_hbm, state.at[2]),
                (grad_hbm, grad), (holder_hbm, holder),
            )
        )
    ]
    loads[0].start()

    barrier = pltpu.get_barrier_semaphore()
    for device in neighbours + peers:
        pl.semaphore_signal(barrier, inc=1, device_id=device, device_id_type=MESH)
    for load in loads[1:]:
        load.start()

    odd = lax.rem(grp, 2) == 1
    sends_near = jnp.logical_or(odd, failed_at[0] == lax.rem(grp + 3, 4))

    def part_copy(src, o, part, kind, device):
        return pltpu.make_async_remote_copy(
            src_ref=src.at[pl.ds(4 * part, 4)],
            dst_ref=recv.at[o, pl.ds(4 * part, 4)],
            send_sem=ex_send.at[PARTS * kind + part],
            recv_sem=ex_recv.at[PARTS * o + part],
            device_id=device,
            device_id_type=MESH,
        )

    first_copies = [part_copy(send.at[0], 0, part, 0, peers[2]) for part in range(PARTS)]
    far_copies = [part_copy(send.at[1], 1, part, 1, peers[1]) for part in range(PARTS)]
    onward_copies = [part_copy(recv.at[0], 1, part, 2, peers[2]) for part in range(PARTS)]
    for part in range(PARTS):
        loads[part].wait()
        for s in range(4 * part, 4 * part + 4):
            for k in range(3):
                near = ckpt[k, s, pl.ds(0, 16, stride=2), :].astype(jnp.bfloat16)
                far = ckpt[k, s, pl.ds(1, 16, stride=2), :].astype(jnp.bfloat16)
                send[0, s, k] = jnp.where(sends_near, near, far)
                send[1, s, k] = far
        if part == 0:
            pl.semaphore_wait(barrier, len(neighbours) + len(peers))
        first_copies[part].start()
        pl.when(odd)(far_copies[part].start)
    for load in loads[PARTS:]:
        load.wait()

    places = []
    seen_near = jnp.int32(0)
    for b in range(16):
        near = holder[0, b] == 1
        places.append((jnp.where(near, 0, 1), jnp.minimum(jnp.where(near, seen_near, b - seen_near), 11)))
        seen_near = seen_near + jnp.where(near, 1, 0)
    failed = failed_at[0] == grp
    for part in range(PARTS):
        first_copies[part].wait_recv()
        pl.when(odd)(onward_copies[part].start)
    for copy in far_copies:
        copy.wait_recv()
    for b, (o, s) in enumerate(places):
        for k in range(3):
            restored[k, pl.ds(64 * (b % 4) + b // 4, 16, stride=4), :] = recv[o, s, k].astype(jnp.float32)
    chosen = [jnp.where(failed, restored[k], state[k]) for k in range(3)]
    new_master, new_first, new_second = adamw_step(*chosen, grad[...].astype(jnp.float32))
    gathered[dp] = new_master.astype(jnp.bfloat16)

    def shard_copy(cell, arrives, direction):
        place = gathered.at[shard_at[cell]]
        return pltpu.make_async_remote_copy(
            src_ref=place,
            dst_ref=place,
            send_sem=ag_send,
            recv_sem=ag_recv.at[arrives],
            device_id=neighbours[direction],
            device_id_type=MESH,
        )

    def place_rows(t):

        for j in range(16):
            shards = [gathered[4 * t + k, 16 * j : 16 * j + 16, :].astype(jnp.float32) for k in range(4)]
            for c in range(4):
                tile = jnp.concatenate([shard[4 * c : 4 * c + 4] for shard in shards], axis=0)
                lanes = 512 * j + 128 * c
                weights[pl.ds(pl.multiple_of(16 * t, 16), 16), lanes : lanes + 128] = tile.astype(jnp.bfloat16)

    def place_lot(low, count):
        def place(i, carry):
            place_rows(i // count * 8 + lax.rem(z + i % count + low, NZ))
            return carry

        lax.fori_loop(0, NX * count, place, 0)

    def in_lot(cell, low, count):
        return (-(cell // 4 % 8) - low) % NZ < count

    lots = [(6, 5), (5, 1), (3, 1), (4, 1)]
    started = max(i for i, (_, _, *directions) in enumerate(TREE) if directions)
    started = max(started, max(i for i, (_, cell, *_) in enumerate(TREE) if in_lot(cell, *lots[0])))
    for _, cell, *directions in TREE[: started + 1]:
        if cell:
            shard_copy(cell, cell, 0).wait_recv()
        for direction in directions:
            shard_copy(cell, moved(cell, direction), direction).start()
        if not cell:
            master_out[...] = new_master
            first_out[...] = new_first
            second_out[...] = new_second
            for copy in first_copies:
                copy.wait_send()

            @pl.when(odd)
            def _():
                for copy in far_copies + onward_copies:
                    copy.wait_send()
    place_lot(*lots[0])
    for lot in lots[1:]:
        for _, cell in TREE[started + 1 :]:
            if in_lot(cell, *lot):
                shard_copy(cell, cell, 0).wait_recv()
        place_lot(*lot)
    everything = gathered.at[pl.ds(0, 127)]
    pltpu.make_async_remote_copy(
        src_ref=everything, dst_ref=everything, send_sem=ag_send, recv_sem=ag_recv.at[0],
        device_id=neighbours[0], device_id_type=MESH,
    ).wait_send()


def output_kernel(*refs):
    copies = [pltpu.make_async_copy(refs[i], refs[i + 4], refs[8].at[i]) for i in range(3)]
    for i in range(8):
        rows = pl.ds(512 // 8 * i, 512 // 8)
        copies.append(pltpu.make_async_copy(refs[3].at[rows], refs[7].at[rows], refs[8].at[3 + i]))
    for copy in copies:
        copy.start()
    for copy in copies:
        copy.wait()


def tiles(rows):
    return rows.reshape(4, 64, 128).transpose(1, 0, 2).reshape(256, 128)


def rows_of(tiled):
    return tiled.reshape(64, 4, 128).transpose(1, 0, 2).reshape(1, 4, 8192)


def per_device(master, first_moment, second_moment, gradient, checkpoints, block_holder, failed_member):
    held = checkpoints.reshape(3, 2, 12, 16, 128).transpose(0, 2, 3, 1, 4).reshape(3, 12, 32, 128)
    operands = [block_holder.reshape(1, 16), held]
    operands += [tiles(value) for value in (master, first_moment, second_moment, gradient)]
    operands = [pltpu.with_memory_space_constraint(value, pltpu.HBM) for value in operands]
    shard = ((256, 128), jnp.float32)
    weights, new_master, new_first, new_second = pl.pallas_call(
        gather_kernel,
        out_shape=[pltpu.VMEM((512, 8192), jnp.bfloat16)] + [pltpu.VMEM(*shard)] * 3,
        in_specs=[pl.BlockSpec(memory_space=pltpu.SMEM)] + [pl.BlockSpec(memory_space=pltpu.HBM)] * 6,
        out_specs=[pl.BlockSpec(memory_space=pltpu.VMEM)] * 4,
        scratch_shapes=[
            pltpu.VMEM((128, 256, 128), jnp.bfloat16),
            pltpu.VMEM((3, 12, 32, 128), jnp.float32),
            pltpu.VMEM((3, 256, 128), jnp.float32),
            pltpu.VMEM((256, 128), jnp.bfloat16),
            pltpu.VMEM((3, 256, 128), jnp.float32),
            pltpu.VMEM((2, 12, 3, 16, 128), jnp.bfloat16),
            pltpu.VMEM((2, 12, 3, 16, 128), jnp.bfloat16),
            pltpu.SMEM((1, 16), jnp.int32),
            pltpu.SemaphoreType.DMA((PARTS + 5,)),
            pltpu.SemaphoreType.DMA((3 * PARTS,)),
            pltpu.SemaphoreType.DMA((2 * PARTS,)),
            pltpu.SemaphoreType.DMA,
            pltpu.SemaphoreType.DMA((128,)),
        ],
        compiler_params=pltpu.CompilerParams(
            collective_id=0, has_side_effects=True, vmem_limit_bytes=24 * 2**20
        ),
        name="restore_step_gather",
    )(failed_member, *operands)
    results = [
        pltpu.with_memory_space_constraint(value, pltpu.VMEM) for value in (new_master, new_first, new_second, weights)
    ]
    new_master, new_first, new_second, weights = pl.pallas_call(
        output_kernel,
        out_shape=[jax.ShapeDtypeStruct(*shard)] * 3 + [jax.ShapeDtypeStruct((512, 8192), jnp.bfloat16)],
        in_specs=[pl.BlockSpec(memory_space=pltpu.VMEM)] * 4,
        out_specs=[pl.BlockSpec(memory_space=pl.ANY)] * 4,
        scratch_shapes=[pltpu.SemaphoreType.DMA((3 + 8,))],
        compiler_params=pltpu.CompilerParams(vmem_limit_bytes=4 * 2**20),
        name="write_outputs",
    )(*results)
    return (rows_of(new_master), rows_of(new_first), rows_of(new_second), weights.reshape(1, 512, 8192))


def solution(mesh):
    return jax.shard_map(
        per_device,
        mesh=mesh,
        in_specs=(
            P("grp", "dp", None),
            P("grp", "dp", None),
            P("grp", "dp", None),
            P("grp", "dp", None),
            P(None, "grp", "dp", None, None, None),
            P("grp", "dp", None),
            P("dp"),
        ),
        out_specs=(
            P("grp", "dp", None),
            P("grp", "dp", None),
            P("grp", "dp", None),
            P("grp", None, None),
        ),
        check_vma=False,
    )
```
